128 devices in a mesh: dp: 8 (over y, z_hi), expert: 16 (over z_lo, x, core).
Axes of the slice: x: 4, y: 4, z: 4 (z_hi: 2, z_lo: 2; z = z_hi * 2 + z_lo), core: 2. Of those that a mesh axis runs over, the one named last changes fastest.
Arguments:
- grad_next: bfloat16 [16384, 4096], P(('dp', 'expert')), may hold values from -6 to 6
- gate_next: float32 [16384, 8], P(('dp', 'expert')), may hold values from 0.05 to 0.5
- expert_ids_next: int32 [16384, 8], P(('dp', 'expert')), may hold values from 0 to 63, all different within a row; in each aligned block of 128 rows (0 to 127, 128 to 255, ...) at most 18 rows name the same one
- hidden_next: bfloat16 [147456, 768], P(('dp', 'expert')), may hold values from -6 to 6
- slot_grads: bfloat16 [147456, 4096], P(('dp', 'expert')), may hold values from -6 to 6
- gate_prev: float32 [16384, 8], P(('dp', 'expert')), may hold values from 0.05 to 0.5
- expert_ids_prev: int32 [16384, 8], P(('dp', 'expert')), may hold values from 0 to 63, all different within a row; in each aligned block of 128 rows (0 to 127, 128 to 255, ...) at most 18 rows name the same one
Outputs:
- down_grad: float32 [64, 768, 4096], P('expert', None, 'dp')
- input_grad: bfloat16 [16384, 4096], P(('dp', 'expert'))
The draws below stay inside these ranges and needn't reach their ends.
Inputs may be any that keep to these rules, and one draw needn't show every extreme that they name: `expert_ids_next`: each row names 8 different experts. In each aligned block of 128 rows (the tokens of one device) no expert is named by more than 18 rows, and some block names some expert exactly 18 times. `expert_ids_prev`: each row names 8 different experts. In each aligned block of 128 rows (the tokens of one device) no expert is named by more than 18 rows, and some block names some expert exactly 18 times.
All inputs are finite; a program needn't handle non-finite values.
Results may differ from the reference program's by a relative error of at most 0.014.
Values may be sent and summed in bfloat16 or wider, within the bound.
No kernel may reach another device: no remote copies, remote signals or barrier semaphores. Data moves between devices by JAX's collectives and lax.ppermute only.
A program may use at most 256 MiB of HBM per device.

```python
import math
import jax
import jax.numpy as jnp
import numpy as np
from jax import lax

D = 4096
FFW = 768
TOP = 8
EXP_DEV = 4
TOK_DEV = 128
GROUPS = 8
SHARDS = 16
EXPERTS = 64
TOKENS = 16384
CAP = 18
ROWS = 147456


def levels(rng, dims, cuts, low, largest):
    loudness = 1.0
    for dim, blocks in cuts:
        heights = jax.random.uniform(jax.random.fold_in(jax.random.fold_in(rng, 6), dim), (blocks,), jnp.float32, low / len(cuts), largest / len(cuts))
        loudness = loudness * jnp.repeat(jnp.exp(heights), dims[dim] // blocks).reshape((-1,) + (1,) * (len(dims) - 1 - dim))
    return loudness


def deal_out(rng, own, number, rows, count, top, most, lean):
    order = jax.random.permutation(rng, count)
    crowded, common = shares(count, rows * top, most, lean, True), shares(count, rows * top, most, lean, False)
    places = jnp.arange(count)

    def named(lengths, turn):
        used = int((lengths > 0).sum())
        fixed = max(1, used // 4)
        moved = fixed + (places - fixed + turn * (used - fixed)) % max(1, count - fixed)
        return jnp.zeros((count,), jnp.int32).at[order[jnp.where(places < fixed, places, moved)]].set(jnp.asarray(lengths, jnp.int32))

    lengths = jnp.where(number % 4 == 0, named(crowded, number // 4), named(common, number - number // 4 - 1))
    mixed = jax.random.permutation(jax.random.fold_in(own, 3), count)
    giver, receiver = mixed[0:count // 2 * 2:2], mixed[1:count // 2 * 2:2]
    margin = jnp.minimum(lengths[giver] - 1, most - lengths[receiver]) // 2
    margin = jnp.where((giver == order[0]) | (receiver == order[0]) | (lengths[receiver] == 0), 0, jnp.maximum(margin, 0))
    moved = jax.random.randint(jax.random.fold_in(own, 4), (count // 2,), 0, 1 << 20) % (margin + 1)
    lengths = lengths.at[giver].add(-moved).at[receiver].add(moved)
    items = jnp.searchsorted(jnp.cumsum(lengths), jnp.arange(rows * top), side="right").astype(jnp.int32)
    table = items.reshape(top, rows).T
    table = table[jax.random.permutation(jax.random.fold_in(own, 1), rows)]
    turn = jax.random.randint(jax.random.fold_in(own, 2), (rows, 1), 0, top)
    return jnp.take_along_axis(table, (jnp.arange(top)[None, :] + turn) % top, axis=1)


def shares(count, total, limit, lean, full):
    weights = [(1 << 20) // math.isqrt(grade ** lean) + 1 for grade in range(1, count + 1)]
    largest = limit if full else min(limit, max(-(-total // count), total * weights[0] // sum(weights)))
    least = 1 if total - largest >= count - 1 else 0
    holding, rest = [largest] + [least] * (count - 1), total - largest - least * (count - 1)
    while rest > 0:
        candidates = [i for i in range(1, count) if holding[i] < largest] or [i for i in range(1, count) if holding[i] < limit]
        mass, remaining = sum([weights[i] for i in candidates]), rest
        for i in candidates:
            more = min(limit - holding[i], max(1, remaining * weights[i] // mass), rest)
            holding[i] = holding[i] + more
            rest = rest - more
    return np.array(holding)


def scatter_about(own_key, dims, deviation, reach, cuts=(), held_as=jnp.bfloat16):
    level = levels(own_key, dims, cuts, -0.22, 0.18) if cuts else 1.0
    values = jax.random.normal(own_key, dims, jnp.float32) * deviation * level
    return jnp.minimum(jnp.maximum(values, -reach), reach).astype(held_as)


def setup_inputs(seed: int = 0) -> dict:
    arg_keys = jax.random.split(jax.random.key(seed), 8)
    grad_next = scatter_about(arg_keys[0], (TOKENS, D), 1.0, 6.0, ((0, 128),))
    gate_next = jnp.clip(jnp.exp(math.log(0.5) - 2.3025851 * jax.random.uniform(arg_keys[1], (TOKENS, TOP), jnp.float32) ** levels(arg_keys[1], (TOKENS, TOP), ((0, 128),), -0.2, 0.2)), 0.05, 0.5)
    expert_ids_next_keys = jax.random.split(jax.random.fold_in(arg_keys[2], 1), TOKENS // TOK_DEV)
    expert_ids_next_turns = jax.random.permutation(jax.random.fold_in(arg_keys[2], 3), TOKENS // TOK_DEV)
    expert_ids_next = jax.vmap(lambda own, number: deal_out(jax.random.fold_in(arg_keys[2], 2), own, number, TOK_DEV, EXPERTS, TOP, CAP, 1))(expert_ids_next_keys, expert_ids_next_turns).reshape((TOKENS, TOP))
    hidden_next = scatter_about(arg_keys[3], (ROWS, FFW), 1.0, 6.0, ((0, 128),))
    slot_grads = scatter_about(arg_keys[4], (ROWS, D), 1.0, 6.0, ((0, 128),))
    gate_prev = jnp.clip(jnp.exp(math.log(0.5) - 2.3025851 * jax.random.uniform(arg_keys[5], (TOKENS, TOP), jnp.float32) ** levels(arg_keys[5], (TOKENS, TOP), ((0, 128),), -0.2, 0.2)), 0.05, 0.5)
    expert_ids_prev_keys = jax.random.split(jax.random.fold_in(arg_keys[6], 1), TOKENS // TOK_DEV)
    expert_ids_prev_turns = jax.random.permutation(jax.random.fold_in(arg_keys[6], 3), TOKENS // TOK_DEV)
    expert_ids_prev = jax.vmap(lambda own, number: deal_out(jax.random.fold_in(arg_keys[6], 2), own, number, TOK_DEV, EXPERTS, TOP, CAP, 1))(expert_ids_prev_keys, expert_ids_prev_turns).reshape((TOKENS, TOP))
    return dict(grad_next=grad_next, gate_next=gate_next, expert_ids_next=expert_ids_next, hidden_next=hidden_next, slot_grads=slot_grads, gate_prev=gate_prev, expert_ids_prev=expert_ids_prev)


def block_ranks(block_ids):
    flat = block_ids.reshape(-1)
    onehot = (flat[:, None] == jnp.arange(EXPERTS, dtype=jnp.int32)[None, :]).astype(jnp.int32)
    before = jnp.cumsum(onehot, axis=0) - onehot
    return jnp.sum(before * onehot, axis=1).astype(jnp.int32)


def slot_index(expert_ids):
    blocks = expert_ids.reshape(GROUPS * SHARDS, TOK_DEV, TOP)
    ranks = jax.vmap(block_ranks)(blocks)
    flat = blocks.reshape(GROUPS * SHARDS, TOK_DEV * TOP)
    block_id = jnp.arange(GROUPS * SHARDS, dtype=jnp.int32)[:, None]
    group = block_id // SHARDS
    source = block_id % SHARDS
    holder = flat // EXP_DEV
    local = flat % EXP_DEV
    index = ((group * SHARDS + holder) * SHARDS + source) * (EXP_DEV * CAP) + local * CAP + ranks
    return index.astype(jnp.int32).reshape(TOKENS, TOP)


def reference(grad_next, gate_next, expert_ids_next, hidden_next, slot_grads, gate_prev, expert_ids_prev):
    group_rows = SHARDS * SHARDS * EXP_DEV * CAP
    group_tokens = SHARDS * TOK_DEV
    slot_next = slot_index(expert_ids_next)

    def group_step(total, group):
        start = (group * group_tokens).astype(jnp.int32)
        grads = lax.dynamic_slice_in_dim(grad_next, start, group_tokens, 0)
        gates = lax.dynamic_slice_in_dim(gate_next, start, group_tokens, 0)
        where = lax.dynamic_slice_in_dim(slot_next, start, group_tokens, 0) - (group * group_rows).astype(jnp.int32)
        scaled = (grads.astype(jnp.float32)[:, None, :] * gates[:, :, None]).astype(jnp.bfloat16).reshape(-1, D)
        sent = jnp.zeros((group_rows, D), jnp.bfloat16).at[where.reshape(-1)].set(scaled)
        hidden = lax.dynamic_slice_in_dim(hidden_next, (group * group_rows).astype(jnp.int32), group_rows, 0)
        sent_five = sent.reshape(SHARDS, SHARDS, EXP_DEV, CAP, D).astype(jnp.float32)
        hidden_five = hidden.reshape(SHARDS, SHARDS, EXP_DEV, CAP, FFW).astype(jnp.float32)
        part = jnp.einsum("dsecf,dsecm->defm", hidden_five, sent_five)
        rounded = lax.optimization_barrier(part.astype(jnp.bfloat16)).astype(jnp.float32)
        return total + rounded.reshape(EXPERTS, FFW, D), None

    start_total = jnp.zeros((EXPERTS, FFW, D), jnp.float32)
    down_grad, _ = lax.scan(group_step, start_total, jnp.arange(GROUPS, dtype=jnp.int32))

    slot_prev = slot_index(expert_ids_prev)

    def combine(pieces):
        rows_index, weights = pieces
        picked = jnp.take(slot_grads, rows_index.reshape(-1), axis=0).astype(jnp.float32).reshape(TOK_DEV, TOP, D)
        return jnp.sum(picked * weights[:, :, None], axis=1).astype(jnp.bfloat16)

    blocks = GROUPS * SHARDS
    input_grad = lax.map(combine, (slot_prev.reshape(blocks, TOK_DEV, TOP), gate_prev.reshape(blocks, TOK_DEV, TOP)))
    return down_grad, input_grad.reshape(TOKENS, D)
```

```python
import functools

import jax
import jax.numpy as jnp
from jax import lax
from jax.experimental import pallas as pl
from jax.experimental.pallas import tpu as pltpu
from jax.sharding import PartitionSpec as P

E = 4
CAP = 18
SLOT = E * CAP
PAIR = 2 * SLOT
TOK = 128
TOP = 8
D = 4096
HALF = D // 2
COLS = 512
FFW = 768
NDP = 8
NEX = 16
X = 4
ROWS = NEX * CAP
SIB = ROWS // 2
LONG = TOK + 16
QUAD = 4
BATCH = 4

VMEM = 56 * 1024 * 1024


def ex_perm(dzl, dx, dc):
    pairs = []
    for zl in range(2):
        for x in range(X):
            for c in range(2):
                src = ((zl ^ dzl) * X + (x + dx) % X) * 2 + (c ^ dc)
                pairs.append((src, (zl * X + x) * 2 + c))
    return pairs


def dp_perm(dy, dzh):
    pairs = []
    for y in range(4):
        for zh in range(2):
            pairs.append((((y + dy) % 4) * 2 + (zh ^ dzh), y * 2 + zh))
    return pairs


def ex_from(value, dzl, dx, dc):
    return lax.ppermute(value, "expert", ex_perm(dzl, dx, dc))


def dp_from(value, dy, dzh):
    return lax.ppermute(value, "dp", dp_perm(dy, dzh))


def slot_weights(lines, first_expert):
    slot = lax.broadcasted_iota(jnp.int32, (SLOT, TOK), 0)
    expert = (
        (slot >= CAP).astype(jnp.int32)
        + (slot >= 2 * CAP).astype(jnp.int32)
        + (slot >= 3 * CAP).astype(jnp.int32)
    )
    place = (slot - CAP * expert).astype(jnp.float32)
    name = (expert + first_expert).astype(jnp.float32)
    gate = jnp.zeros((SLOT, TOK), jnp.float32)
    named = jnp.zeros((SLOT, TOK), jnp.float32)
    for k in range(TOP):
        same = lines[k] == name
        named = jnp.where(same, 1.0, named)
        gate = jnp.where(same, lines[TOP + k], gate)
    earlier = (
        lax.broadcasted_iota(jnp.int32, (TOK, TOK), 0)
        < lax.broadcasted_iota(jnp.int32, (TOK, TOK), 1)
    ).astype(jnp.bfloat16)
    rank = jnp.dot(named.astype(jnp.bfloat16), earlier, preferred_element_type=jnp.float32)
    return jnp.where(rank == place, gate, 0.0)


def cut_columns_kernel(targets, grad_ref, meta_ref, *out_refs):
    table = meta_ref[2 * TOP :, :].astype(jnp.bfloat16)
    table = jnp.concatenate([table, jnp.zeros((2 * TOP, COLS - TOK), jnp.bfloat16)], axis=1)
    outs = [ref.at[dy] for ref in out_refs for dy in range(4)]
    for i, out in enumerate(outs):
        at = pl.multiple_of(targets[i] * COLS, COLS)
        out[:TOK, :] = grad_ref[:, pl.ds(at, COLS)]
        out[TOK:, :] = table


def cut_columns(targets, grad, meta):
    shapes = [(4, LONG, COLS)] * 2
    return pl.pallas_call(
        cut_columns_kernel,
        grid_spec=pltpu.PrefetchScalarGridSpec(
            num_scalar_prefetch=1,
            grid=(1,),
            in_specs=[
                pl.BlockSpec((TOK, D), lambda i, s: (0, 0)),
                pl.BlockSpec((4 * TOP, TOK), lambda i, s: (0, 0)),
            ],
            out_specs=[pl.BlockSpec(s, lambda i, _, n=len(s): (0,) * n) for s in shapes],
        ),
        out_shape=[jax.ShapeDtypeStruct(s, jnp.bfloat16) for s in shapes],
        compiler_params=pltpu.CompilerParams(vmem_limit_bytes=VMEM),
    )(targets, grad, meta)


def return_route_kernel(scalars, meta_ref, out_ref):
    core = scalars[0]
    for i in range(8):
        lines = [meta_ref[i, k : k + 1, :] for k in range(2 * TOP)]
        for j in range(2):
            gate = slot_weights(lines, scalars[1 + j])
            none = jnp.zeros_like(gate)
            both = jnp.concatenate(
                [jnp.where(core == 0, gate, none), jnp.where(core == 1, gate, none)], axis=0
            )
            out_ref[i, j] = both.astype(jnp.bfloat16)


def return_route(scalars, meta):
    return pl.pallas_call(
        return_route_kernel,
        grid_spec=pltpu.PrefetchScalarGridSpec(
            num_scalar_prefetch=1,
            grid=(1,),
            in_specs=[pl.BlockSpec((8, 2 * TOP, TOK), lambda i, s: (0, 0, 0))],
            out_specs=pl.BlockSpec((8, 2, PAIR, TOK), lambda i, s: (0, 0, 0, 0)),
        ),
        out_shape=jax.ShapeDtypeStruct((8, 2, PAIR, TOK), jnp.bfloat16),
        compiler_params=pltpu.CompilerParams(vmem_limit_bytes=VMEM),
    )(scalars, meta)


def combine_kernel(scalars, weight_ref, own_ref, sib_ref, *out_refs, outs):
    chunk = 1024
    for at in range(0, D, chunk):
        total = jnp.zeros((TOK, chunk), jnp.float32)
        for j, rows in enumerate((own_ref, sib_ref)):
            total += lax.dot_general(
                weight_ref[0, j],
                rows[:, at : at + chunk],
                (((0,), (0,)), ((), ())),
                preferred_element_type=jnp.float32,
            )
        for (low, high), ref in zip(outs, out_refs):
            if low <= at < high:
                ref[0, :, at - low : at - low + chunk] = total.astype(jnp.bfloat16)


def combine(pairs, weights, own, sib, first, steps, outs):
    out_specs = [pl.BlockSpec((1, TOK, high - low), lambda i, s: (i, 0, 0)) for low, high in outs]
    return pl.pallas_call(
        functools.partial(combine_kernel, outs=outs),
        grid_spec=pltpu.PrefetchScalarGridSpec(
            num_scalar_prefetch=1,
            grid=(steps,),
            in_specs=[
                pl.BlockSpec((1, 2, PAIR, TOK), lambda i, s: (first + i, 0, 0, 0)),
                pl.BlockSpec((PAIR, D), lambda i, s: (s[first + i], 0)),
                pl.BlockSpec((PAIR, D), lambda i, s: (s[first + i], 0)),
            ],
            out_specs=out_specs,
        ),
        out_shape=[
            jax.ShapeDtypeStruct((steps, TOK, high - low), jnp.bfloat16) for low, high in outs
        ],
        compiler_params=pltpu.CompilerParams(vmem_limit_bytes=VMEM),
    )(pairs, weights, own, sib)


def sent_kernel(scalars, spread_ref, *refs):
    tok_refs, out_ref = refs[:8], refs[8]
    quads = []
    for quad in range(2):
        route = []
        for i in range(QUAD):
            table = tok_refs[quad * QUAD + i][0, TOK:, :TOK].astype(jnp.float32)
            lines = [table[k : k + 1, :] for k in range(2 * TOP)]
            gate = slot_weights(lines, scalars[0]).astype(jnp.bfloat16)
            rows = jnp.dot(spread_ref[i], gate, preferred_element_type=jnp.float32)
            route.append(rows.astype(jnp.bfloat16))
        tokens = jnp.concatenate(
            [tok_refs[quad * QUAD + i][0, :TOK, :] for i in range(QUAD)], axis=0
        )
        quads.append(
            jnp.dot(
                jnp.concatenate(route, axis=1), tokens, preferred_element_type=jnp.float32
            )
        )
    for e in range(E):
        rows = [quad[e * SLOT : (e + 1) * SLOT, :] for quad in quads]
        out_ref[0, e] = jnp.concatenate(rows, axis=0).astype(jnp.bfloat16)


def build_sent(scalars, spread, tokens):
    return pl.pallas_call(
        sent_kernel,
        grid_spec=pltpu.PrefetchScalarGridSpec(
            num_scalar_prefetch=1,
            grid=(NDP,),
            in_specs=[pl.BlockSpec((QUAD, QUAD * SLOT, SLOT), lambda g, s: (0, 0, 0))]
            + [pl.BlockSpec((1, LONG, COLS), lambda g, s: (g, 0, 0)) for _ in range(8)],
            out_specs=pl.BlockSpec((1, E, SIB, COLS), lambda g, s: (g, 0, 0, 0)),
        ),
        out_shape=jax.ShapeDtypeStruct((NDP, E, SIB, COLS), jnp.bfloat16),
        compiler_params=pltpu.CompilerParams(vmem_limit_bytes=VMEM),
    )(scalars, spread, *tokens)


def weight_kernel(near_ref, far_ref, zero_ref, one_ref, low_ref, high_ref, three_ref, *refs):
    out_ref = refs[-1]
    two = jnp.where(pl.program_id(0) < E // 2, low_ref[0], high_ref[0])
    hidden = jnp.concatenate([zero_ref[0], one_ref[0], two, three_ref[0]], axis=0)
    sent = jnp.concatenate(
        [ref[g, 0] for g in range(BATCH) for ref in (near_ref, far_ref)], axis=0
    )
    total = lax.dot_general(
        hidden, sent, (((0,), (0,)), ((), ())), preferred_element_type=jnp.float32
    )
    if len(refs) > 1:
        total += refs[0][0]
    out_ref[0] = total


def weight_grad(sents, batch, hiddens, before):
    result = pl.BlockSpec((1, FFW, COLS), lambda e: (e, 0, 0))
    rows = pl.BlockSpec((1, ROWS, FFW), lambda e: (e, 0, 0))
    return pl.pallas_call(
        weight_kernel,
        grid=(E,),
        in_specs=[
            pl.BlockSpec((BATCH, 1, SIB, COLS), lambda e: (batch, e, 0, 0)),
            pl.BlockSpec((BATCH, 1, SIB, COLS), lambda e: (batch, e, 0, 0)),
            rows,
            rows,
            pl.BlockSpec((1, ROWS, FFW), lambda e: (jnp.minimum(e, E // 2 - 1), 0, 0)),
            pl.BlockSpec((1, ROWS, FFW), lambda e: (jnp.maximum(e - E // 2, 0), 0, 0)),
            rows,
        ]
        + [result] * len(before),
        out_specs=result,
        out_shape=jax.ShapeDtypeStruct((E, FFW, COLS), jnp.float32),
        compiler_params=pltpu.CompilerParams(vmem_limit_bytes=VMEM),
    )(*sents, *hiddens, *before)


def local(
    grad_next, gate_next, expert_ids_next, hidden_next, slot_grads, gate_prev, expert_ids_prev
):
    me = lax.axis_index("expert")
    zl, x, c = me // (2 * X), (me // 2) % X, me % 2
    dp = lax.axis_index("dp")
    y, zh = dp // 2, dp % 2
    first = (me * E).astype(jnp.int32)

    meta = jnp.concatenate(
        [
            expert_ids_prev.astype(jnp.float32),
            gate_prev,
            expert_ids_next.astype(jnp.float32),
            gate_next,
        ],
        axis=1,
    ).T

    targets = [((y - dy) % 4) * 2 + z for z in (zh, 1 - zh) for dy in range(4)]
    same, other = cut_columns(jnp.stack(targets).astype(jnp.int32), grad_next, meta)
    other = dp_from(other, 0, 1)
    meta = meta[: 2 * TOP]
    meta = jnp.stack([meta, ex_from(meta, 1, 0, 0)])
    meta = jnp.stack([meta] + [ex_from(meta, 0, dx, 0) for dx in (1, 2, 3)])
    meta_prev = meta.reshape(8, 2 * TOP, TOK)

    sibling = ex_from(slot_grads, 0, 0, 1)
    weights = return_route(
        jnp.stack([c, first, (me ^ 1) * E]).astype(jnp.int32), meta_prev
    )
    pairs = jnp.stack(
        [(zl ^ dzl) * X + (x + dx) % X for dx in range(X) for dzl in range(2)]
    ).astype(jnp.int32)
    halves = [(0, HALF), (HALF, D)]

    def part(dx):
        return combine(pairs, weights, slot_grads, sibling, 2 * dx, 2, halves)

    def add(*values):
        return sum(v.astype(jnp.float32) for v in values).astype(jnp.bfloat16)

    def after(value, *earlier):
        return lax.optimization_barrier((value, earlier))[0]

    left, right = part(2)
    both = after(jnp.stack([same, other], axis=1), left, right)
    own = [both[0]] + [dp_from(both[dy], dy, 0) for dy in (1, 2, 3)]
    own = jnp.stack(own, axis=1).reshape(NDP, LONG, COLS)
    left, right = ex_from(left, 0, 3, 0), ex_from(right, 0, 1, 0)
    up, down, here = part(1), part(3), part(0)

    blocks = jnp.stack(
        [
            ((zl ^ dzl) * X + (x + dx) % X) * 2 + (c ^ dc)
            for dzl in range(2)
            for dc in range(2)
            for dx in range(X)
        ]
    ).reshape(1, NEX, 1)
    source = (
        blocks * SLOT
        + jnp.arange(E, dtype=jnp.int32)[:, None, None] * CAP
        + jnp.arange(CAP, dtype=jnp.int32)[None, None, :]
    ).reshape(-1)
    move = (source[:, None] == jnp.arange(NEX * SLOT, dtype=jnp.int32)[None, :]).astype(
        jnp.bfloat16
    )
    mine = jnp.dot(move, hidden_next, preferred_element_type=jnp.float32).astype(jnp.bfloat16)
    mine = after(mine.reshape(E, ROWS, FFW), own)

    def to_sides(zero):
        return dp_from(zero, 1, 0), dp_from(zero, 3, 0)

    def onward(one, three):
        return dp_from(one[: E // 2], 1, 0), dp_from(three[E // 2 :], 3, 0)

    one, three = to_sides(mine)
    low, high = onward(one, three)

    over = ex_from(own, 1, 0, 0)
    across = dp_from(after(mine, over), 0, 1)
    own = after(own, left, right)
    near = [own, ex_from(own, 0, 1, 0), None, ex_from(own, 0, 3, 0)]
    near[2] = jnp.concatenate(
        [ex_from(near[1][:BATCH], 0, 1, 0), ex_from(near[3][BATCH:], 0, 3, 0)]
    )
    over_late = after(over, near[2], one, three)
    far = [
        over,
        ex_from(over_late, 0, 1, 0),
        ex_from(after(near[2], across), 1, 0, 0),
        ex_from(over_late, 0, 3, 0),
    ]
    near = near[:1] + near[1:] + [ex_from(t, 0, 0, 1) for t in near]
    far_all = far + [ex_from(t, 0, 0, 1) for t in far]

    across = after(across, low, high)
    across_one, across_three = to_sides(across)
    across_low, across_high = onward(across_one, across_three)

    up = [add(up[0], left), up[1]]
    down = [down[0], add(down[1], right)]
    row = jnp.arange(QUAD * SLOT, dtype=jnp.int32)[None, :, None]
    slot = jnp.arange(SLOT, dtype=jnp.int32)[None, None, :]
    block = jnp.arange(QUAD, dtype=jnp.int32)[:, None, None]
    spread = (
        (row % SLOT // CAP == block) & (row // SLOT * CAP + row % CAP == slot)
    ).astype(jnp.bfloat16)
    crossed, sents = [], []
    gates = [(far[1], far[3], across, low, high, *near), (far[2], *far_all)]
    for i in range(2):
        u = ex_from(after(up[i], *gates[i], *sents), 0, 3, 0)
        d = ex_from(after(down[i], *gates[i], *sents), 0, 1, 0)
        sents.append(build_sent(first[None], spread, (near, far_all)[i]))
        side = add(here[i][1], u[1], d[1])
        if i:
            side = after(side, *sents)
        side = ex_from(side, 1, 0, 0)
        crossed.append(add(here[i][0], u[0], d[0], side))
    input_grad = jnp.concatenate(crossed, axis=1)
    down_grad = weight_grad(sents, 0, (mine, one, low, high, three), [])
    down_grad = weight_grad(
        sents, 1, (across, across_one, across_low, across_high, across_three), [down_grad]
    )
    return down_grad, input_grad


def solution(mesh):
    rows = P(("dp", "expert"), None)
    return jax.shard_map(
        local,
        mesh=mesh,
        in_specs=(rows,) * 7,
        out_specs=(P("expert", None, "dp"), rows),
        check_vma=False,
    )
```

```python
import functools

import jax
import jax.numpy as jnp
from jax import lax
from jax.experimental import pallas as pl
from jax.experimental.pallas import tpu as pltpu
from jax.sharding import PartitionSpec as P

E = 4
CAP = 18
SLOT = E * CAP
PAIR = 2 * SLOT
TOK = 128
TOP = 8
D = 4096
HALF = D // 2
COLS = 512
FFW = 768
NDP = 8
NEX = 16
X = 4
ROWS = NEX * CAP
LONG = TOK + 16
QUAD = 4
BATCH = 4

VMEM = 56 * 1024 * 1024


def ex_perm(dzl, dx, dc):
    pairs = []
    for zl in range(2):
        for x in range(X):
            for c in range(2):
                src = ((zl ^ dzl) * X + (x + dx) % X) * 2 + (c ^ dc)
                pairs.append((src, (zl * X + x) * 2 + c))
    return pairs


def dp_perm(dy, dzh):
    pairs = []
    for y in range(4):
        for zh in range(2):
            pairs.append((((y + dy) % 4) * 2 + (zh ^ dzh), y * 2 + zh))
    return pairs


def ex_from(value, dzl, dx, dc):
    return lax.ppermute(value, "expert", ex_perm(dzl, dx, dc))


def dp_from(value, dy, dzh):
    return lax.ppermute(value, "dp", dp_perm(dy, dzh))


def slot_weights(blocks):
    slot = lax.broadcasted_iota(jnp.int32, (SLOT, TOK), 0)
    expert = (
        (slot >= CAP).astype(jnp.int32)
        + (slot >= 2 * CAP).astype(jnp.int32)
        + (slot >= 3 * CAP).astype(jnp.int32)
    )
    place = (slot - CAP * expert).astype(jnp.float32)
    gates = []
    for lines, first_expert in blocks:
        name = (expert + first_expert).astype(jnp.float32)
        gate = jnp.zeros((SLOT, TOK), jnp.float32)
        for k in range(TOP):
            gate = jnp.where(lines[k] == name, lines[TOP + k], gate)
        gates.append(gate)
    earlier = (
        lax.broadcasted_iota(jnp.int32, (TOK, TOK), 0)
        < lax.broadcasted_iota(jnp.int32, (TOK, TOK), 1)
    ).astype(jnp.bfloat16)
    named = jnp.concatenate([(gate > 0.0).astype(jnp.float32) for gate in gates], axis=0)
    rank = jnp.dot(named.astype(jnp.bfloat16), earlier, preferred_element_type=jnp.float32)
    return [
        jnp.where(rank[i * SLOT : (i + 1) * SLOT] == place, gate, 0.0)
        for i, gate in enumerate(gates)
    ]


def cut_columns_kernel(targets, grad_ref, meta_ref, *out_refs):
    table = meta_ref[2 * TOP :, :].astype(jnp.bfloat16)
    table = jnp.concatenate([table, jnp.zeros((2 * TOP, COLS - TOK), jnp.bfloat16)], axis=1)
    outs = [ref.at[dy] for ref in out_refs for dy in range(4)]
    for i, out in enumerate(outs):
        at = pl.multiple_of(targets[i] * COLS, COLS)
        out[:TOK, :] = grad_ref[:, pl.ds(at, COLS)]
        out[TOK:, :] = table


def cut_columns(targets, grad, meta):
    shapes = [(4, LONG, COLS)] * 2
    return pl.pallas_call(
        cut_columns_kernel,
        grid_spec=pltpu.PrefetchScalarGridSpec(
            num_scalar_prefetch=1,
            grid=(1,),
            in_specs=[
                pl.BlockSpec((TOK, D), lambda i, s: (0, 0)),
                pl.BlockSpec((4 * TOP, TOK), lambda i, s: (0, 0)),
            ],
            out_specs=[pl.BlockSpec(s, lambda i, _, n=len(s): (0,) * n) for s in shapes],
        ),
        out_shape=[jax.ShapeDtypeStruct(s, jnp.bfloat16) for s in shapes],
        compiler_params=pltpu.CompilerParams(vmem_limit_bytes=VMEM),
    )(targets, grad, meta)


def return_route_kernel(scalars, meta_ref, out_ref):
    core = scalars[0]
    blocks = []
    for i in range(8):
        lines = [meta_ref[i, k : k + 1, :] for k in range(2 * TOP)]
        blocks += [(lines, scalars[1]), (lines, scalars[2])]
    for n, gate in enumerate(slot_weights(blocks)):
        none = jnp.zeros_like(gate)
        both = jnp.concatenate(
            [jnp.where(core == 0, gate, none), jnp.where(core == 1, gate, none)], axis=0
        )
        out_ref[n // 2, n % 2] = both.astype(jnp.bfloat16)


def return_route(scalars, meta):
    return pl.pallas_call(
        return_route_kernel,
        grid_spec=pltpu.PrefetchScalarGridSpec(
            num_scalar_prefetch=1,
            grid=(1,),
            in_specs=[pl.BlockSpec((8, 2 * TOP, TOK), lambda i, s: (0, 0, 0))],
            out_specs=pl.BlockSpec((8, 2, PAIR, TOK), lambda i, s: (0, 0, 0, 0)),
        ),
        out_shape=jax.ShapeDtypeStruct((8, 2, PAIR, TOK), jnp.bfloat16),
        compiler_params=pltpu.CompilerParams(vmem_limit_bytes=VMEM),
    )(scalars, meta)


def combine_kernel(scalars, weight_ref, own_ref, sib_ref, *out_refs, outs):
    chunk = 1024
    for at in range(0, D, chunk):
        total = jnp.zeros((TOK, chunk), jnp.float32)
        for j, rows in enumerate((own_ref, sib_ref)):
            total += lax.dot_general(
                weight_ref[0, j],
                rows[:, at : at + chunk],
                (((0,), (0,)), ((), ())),
                preferred_element_type=jnp.float32,
            )
        for (low, high), ref in zip(outs, out_refs):
            if low <= at < high:
                ref[0, :, at - low : at - low + chunk] = total.astype(jnp.bfloat16)


def combine(pairs, weights, own, sib, first, steps, outs):
    out_specs = [pl.BlockSpec((1, TOK, high - low), lambda i, s: (i, 0, 0)) for low, high in outs]
    return pl.pallas_call(
        functools.partial(combine_kernel, outs=outs),
        grid_spec=pltpu.PrefetchScalarGridSpec(
            num_scalar_prefetch=1,
            grid=(steps,),
            in_specs=[
                pl.BlockSpec((1, 2, PAIR, TOK), lambda i, s: (first + i, 0, 0, 0)),
                pl.BlockSpec((PAIR, D), lambda i, s: (s[first + i], 0)),
                pl.BlockSpec((PAIR, D), lambda i, s: (s[first + i], 0)),
            ],
            out_specs=out_specs,
        ),
        out_shape=[
            jax.ShapeDtypeStruct((steps, TOK, high - low), jnp.bfloat16) for low, high in outs
        ],
        compiler_params=pltpu.CompilerParams(vmem_limit_bytes=VMEM),
    )(pairs, weights, own, sib)


def sent_kernel(scalars, order_ref, *refs):
    tok_refs, out_refs = refs[:QUAD], refs[QUAD:]
    tokens = jnp.concatenate([ref[0, :TOK, :] for ref in tok_refs], axis=0)
    blocks = []
    for j in range(2):
        for ref in tok_refs:
            table = ref[0, TOK:, :TOK].astype(jnp.float32)
            blocks.append(([table[k : k + 1, :] for k in range(2 * TOP)], scalars[j]))
    gates = slot_weights(blocks)
    none = jnp.zeros((SLOT, TOK), jnp.float32)
    for j, out_ref in enumerate(out_refs):
        route = [
            jnp.concatenate(
                [gates[j * QUAD + i] if i == n else none for n in range(QUAD)], axis=1
            )
            for i in range(QUAD)
        ]
        route = jnp.concatenate(route, axis=0).astype(jnp.bfloat16)
        route = jnp.dot(order_ref[...], route, preferred_element_type=jnp.float32)
        sent = jnp.dot(route.astype(jnp.bfloat16), tokens, preferred_element_type=jnp.float32)
        for e in range(E):
            out_ref[0, e] = sent[e * SLOT : (e + 1) * SLOT, :].astype(jnp.bfloat16)


def build_sent(scalars, order, tokens):
    rows = (NDP, E, SLOT, COLS)
    return pl.pallas_call(
        sent_kernel,
        grid_spec=pltpu.PrefetchScalarGridSpec(
            num_scalar_prefetch=1,
            grid=(NDP,),
            in_specs=[pl.BlockSpec((QUAD * SLOT, QUAD * SLOT), lambda g, s: (0, 0))]
            + [pl.BlockSpec((1, LONG, COLS), lambda g, s: (g, 0, 0)) for _ in range(QUAD)],
            out_specs=[pl.BlockSpec((1,) + rows[1:], lambda g, s: (g, 0, 0, 0))] * 2,
        ),
        out_shape=[jax.ShapeDtypeStruct(rows, jnp.bfloat16)] * 2,
        compiler_params=pltpu.CompilerParams(vmem_limit_bytes=VMEM),
        cost_estimate=pl.CostEstimate(
            flops=14_000_000_000, bytes_accessed=15_000_000, transcendentals=0
        ),
    )(scalars, order, *tokens)


def weight_kernel(*refs, counts):
    sent_refs, refs = refs[:4], refs[4:]
    hidden = []
    for count in counts:
        part, refs = refs[:count], refs[count:]
        if count == 2:
            hidden.append(jnp.where(pl.program_id(0) < E // 2, part[0][0], part[1][0]))
        else:
            hidden.append(part[0][0])
    hidden = jnp.concatenate(hidden, axis=0)
    sent = [ref[g, 0].astype(jnp.float32) for g in range(BATCH) for ref in sent_refs]
    sent = jnp.concatenate(sent, axis=0).astype(jnp.bfloat16)
    total = lax.dot_general(
        hidden, sent, (((0,), (0,)), ((), ())), preferred_element_type=jnp.float32
    )
    if len(refs) > 1:
        total += refs[0][0]
    refs[-1][0] = total


def weight_grad(sents, batch, sources, before):
    result = pl.BlockSpec((1, FFW, COLS), lambda e: (e, 0, 0))
    whole = pl.BlockSpec((1, ROWS, FFW), lambda e: (e, 0, 0))
    halves = [
        pl.BlockSpec((1, ROWS, FFW), lambda e: (jnp.minimum(e, E // 2 - 1), 0, 0)),
        pl.BlockSpec((1, ROWS, FFW), lambda e: (jnp.maximum(e - E // 2, 0), 0, 0)),
    ]
    specs = [spec for s in sources for spec in (halves if len(s) == 2 else [whole])]
    return pl.pallas_call(
        functools.partial(weight_kernel, counts=tuple(len(s) for s in sources)),
        grid=(E,),
        in_specs=[pl.BlockSpec((BATCH, 1, SLOT, COLS), lambda e: (batch, e, 0, 0))] * 4
        + specs
        + [result] * len(before),
        out_specs=result,
        out_shape=jax.ShapeDtypeStruct((E, FFW, COLS), jnp.float32),
        compiler_params=pltpu.CompilerParams(vmem_limit_bytes=VMEM),
        cost_estimate=pl.CostEstimate(
            flops=11_000_000_000, bytes_accessed=20_000_000, transcendentals=0
        ),
    )(*sents, *[a for s in sources for a in s], *before)


def local(
    grad_next, gate_next, expert_ids_next, hidden_next, slot_grads, gate_prev, expert_ids_prev
):
    me = lax.axis_index("expert")
    zl, x, c = me // (2 * X), (me // 2) % X, me % 2
    dp = lax.axis_index("dp")
    y, zh = dp // 2, dp % 2
    first = (me * E).astype(jnp.int32)

    def after(value, *earlier):
        return lax.optimization_barrier((value, earlier))[0]

    meta = jnp.concatenate(
        [
            expert_ids_prev.astype(jnp.float32),
            gate_prev,
            expert_ids_next.astype(jnp.float32),
            gate_next,
        ],
        axis=1,
    ).T

    targets = [((y - dy) % 4) * 2 + z for z in (zh, 1 - zh) for dy in range(4)]
    same, other = cut_columns(jnp.stack(targets).astype(jnp.int32), grad_next, meta)
    other = dp_from(other, 0, 1)

    meta = meta[: 2 * TOP]
    meta = jnp.stack([meta, ex_from(meta, 1, 0, 0)])
    meta = jnp.stack([meta] + [ex_from(meta, 0, dx, 0) for dx in (1, 2, 3)])
    meta_prev = meta.reshape(8, 2 * TOP, TOK)

    sibling = ex_from(slot_grads, 0, 0, 1)
    weights = return_route(
        jnp.stack([c, first, (me ^ 1) * E]).astype(jnp.int32), meta_prev
    )
    pairs = jnp.stack(
        [(zl ^ dzl) * X + (x + dx) % X for dx in range(X) for dzl in range(2)]
    ).astype(jnp.int32)
    halves = [(0, HALF), (HALF, D)]

    def part(dx):
        return combine(pairs, weights, slot_grads, sibling, 2 * dx, 2, halves)

    def add(*values):
        return sum(v.astype(jnp.float32) for v in values).astype(jnp.bfloat16)

    blocks = jnp.stack(
        [
            ((zl ^ dzl) * X + (x + dx) % X) * 2 + (c ^ dc)
            for dzl in range(2)
            for dc in range(2)
            for dx in range(X)
        ]
    ).reshape(1, NEX, 1)
    source = (
        blocks * SLOT
        + jnp.arange(E, dtype=jnp.int32)[:, None, None] * CAP
        + jnp.arange(CAP, dtype=jnp.int32)[None, None, :]
    ).reshape(-1)
    move = (source[:, None] == jnp.arange(NEX * SLOT, dtype=jnp.int32)[None, :]).astype(
        jnp.bfloat16
    )
    mine = jnp.dot(move, hidden_next, preferred_element_type=jnp.float32).astype(jnp.bfloat16)
    mine = mine.reshape(E, ROWS, FFW)

    left, right = part(2)
    both = after(jnp.stack([same, other], axis=1), left, right)
    own = [both[0]] + [dp_from(both[dy], dy, 0) for dy in (1, 2, 3)]
    left, right = ex_from(left, 0, 3, 0), ex_from(right, 0, 1, 0)
    up, down, here = part(1), part(3), part(0)
    own = after(own, left, right, *up, *down, *here)
    own = jnp.stack(own, axis=1).reshape(NDP, LONG, COLS)
    up = [add(up[0], left), up[1]]
    down = [down[0], add(down[1], right)]

    def to_sides(zero):
        return dp_from(zero, 1, 0), dp_from(zero, 3, 0)

    mine_low, mine_high = mine[: E // 2], mine[E // 2 :]
    low_near = to_sides(after(mine_low, own))
    high_near = to_sides(after(mine_high, *low_near))
    near_onward = after((low_near[0], high_near[1]), *low_near, *high_near)
    near_onward = dp_from(near_onward[0], 1, 0), dp_from(near_onward[1], 3, 0)

    over = ex_from(own, 1, 0, 0)
    across_low = dp_from(after(mine_low, over), 0, 1)
    near = [own, ex_from(own, 0, 1, 0), None, ex_from(own, 0, 3, 0)]
    near[2] = jnp.concatenate(
        [
            ex_from(after(near[1][:BATCH], over, *up, *down, *low_near), 0, 1, 0),
            ex_from(after(near[3][BATCH:], over, *up, *down, *low_near), 0, 3, 0),
        ]
    )
    to = jnp.arange(QUAD * SLOT, dtype=jnp.int32)
    block_row = to % SLOT // CAP * SLOT + to // SLOT * CAP + to % CAP
    order = (block_row[:, None] == to[None, :]).astype(jnp.bfloat16)
    both_first = jnp.stack([first, (me ^ 1) * E]).astype(jnp.int32)

    def slot_rows(tokens):
        mine_rows, theirs = build_sent(both_first, order, tokens)
        return [mine_rows, ex_from(theirs, 0, 0, 1)]

    sents = slot_rows(after(near, *high_near))
    over_late = after(over, near[2])
    far = [
        over,
        ex_from(over_late, 0, 1, 0),
        ex_from(after(near[2], across_low), 1, 0, 0),
        ex_from(over_late, 0, 3, 0),
    ]

    across_high = dp_from(after(mine_high, far[2]), 0, 1)
    low_far = to_sides(after(across_low, *near_onward))
    high_far = to_sides(after(across_high, *low_far))
    far_onward = after((low_far[0], high_far[1]), *low_far, *high_far)
    far_onward = dp_from(far_onward[0], 1, 0), dp_from(far_onward[1], 3, 0)

    crossed = []
    gates = [(far[1], far[3], *near_onward), low_far]
    for i in range(2):
        if i:
            sents = sents + slot_rows(far)
        u = ex_from(after(up[i], *gates[i], *sents), 0, 3, 0)
        d = ex_from(after(down[i], *gates[i], *sents), 0, 1, 0)
        gates[1] += (u, d)
        side = add(here[i][1], u[1], d[1])
        if i:
            sources = [(mine_low, mine_high), *zip(low_near, high_near)]
            sources.insert(2, near_onward)
            down_grad = weight_grad(sents, 0, sources, [])
            side = after(side, down_grad, *high_far)
        side = ex_from(side, 1, 0, 0)
        crossed.append(add(here[i][0], u[0], d[0], side))
    input_grad = jnp.concatenate(crossed, axis=1)
    sources = [(across_low, across_high), *zip(low_far, high_far)]
    sources.insert(2, far_onward)
    down_grad = weight_grad(sents, 1, sources, [down_grad])
    return down_grad, input_grad


def solution(mesh):
    rows = P(("dp", "expert"), None)
    return jax.shard_map(
        local,
        mesh=mesh,
        in_specs=(rows,) * 7,
        out_specs=(P("expert", None, "dp"), rows),
        check_vma=False,
    )
```

```python
import functools

import jax
import jax.numpy as jnp
from jax import lax
from jax.experimental import pallas as pl
from jax.experimental.pallas import tpu as pltpu
from jax.sharding import PartitionSpec as P

E = 4
CAP = 18
SLOT = E * CAP
PAIR = 2 * SLOT
TOK = 128
TOP = 8
D = 4096
HALF = D // 2
COLS = 512
FFW = 768
NDP = 8
NEX = 16
X = 4
ROWS = NEX * CAP
LONG = TOK + 16
QUAD = 4
BATCH = 4
STEP = 2

VMEM = 56 * 1024 * 1024


def ex_perm(dzl, dx, dc):
    pairs = []
    for zl in range(2):
        for x in range(X):
            for c in range(2):
                src = ((zl ^ dzl) * X + (x + dx) % X) * 2 + (c ^ dc)
                pairs.append((src, (zl * X + x) * 2 + c))
    return pairs


def dp_perm(dy, dzh):
    pairs = []
    for y in range(4):
        for zh in range(2):
            pairs.append((((y + dy) % 4) * 2 + (zh ^ dzh), y * 2 + zh))
    return pairs


def ex_from(value, dzl, dx, dc):
    return lax.ppermute(value, "expert", ex_perm(dzl, dx, dc))


def dp_from(value, dy, dzh):
    return lax.ppermute(value, "dp", dp_perm(dy, dzh))


def slot_weights(blocks):
    slot = lax.broadcasted_iota(jnp.int32, (SLOT, TOK), 0)
    expert = (
        (slot >= CAP).astype(jnp.int32)
        + (slot >= 2 * CAP).astype(jnp.int32)
        + (slot >= 3 * CAP).astype(jnp.int32)
    )
    place = (slot - CAP * expert).astype(jnp.float32)
    gates = []
    for lines, first_expert in blocks:
        name = (expert + first_expert).astype(jnp.float32)
        gate = jnp.zeros((SLOT, TOK), jnp.float32)
        for k in range(TOP):
            gate = jnp.where(lines[k] == name, lines[TOP + k], gate)
        gates.append(gate)
    earlier = (
        lax.broadcasted_iota(jnp.int32, (TOK, TOK), 0)
        < lax.broadcasted_iota(jnp.int32, (TOK, TOK), 1)
    ).astype(jnp.bfloat16)
    named = jnp.concatenate([(gate > 0.0).astype(jnp.float32) for gate in gates], axis=0)
    rank = jnp.dot(named.astype(jnp.bfloat16), earlier, preferred_element_type=jnp.float32)
    return [
        jnp.where(rank[i * SLOT : (i + 1) * SLOT] == place, gate, 0.0)
        for i, gate in enumerate(gates)
    ]


def cut_columns_kernel(targets, grad_ref, meta_ref, *out_refs):
    table = meta_ref[2 * TOP :, :].astype(jnp.bfloat16)
    table = jnp.concatenate([table, jnp.zeros((2 * TOP, COLS - TOK), jnp.bfloat16)], axis=1)
    outs = [ref.at[dy] for ref in out_refs for dy in range(4)]
    for i, out in enumerate(outs):
        at = pl.multiple_of(targets[i] * COLS, COLS)
        out[:TOK, :] = grad_ref[:, pl.ds(at, COLS)]
        out[TOK:, :] = table


def cut_columns(targets, grad, meta):
    shapes = [(4, LONG, COLS)] * 2
    return pl.pallas_call(
        cut_columns_kernel,
        grid_spec=pltpu.PrefetchScalarGridSpec(
            num_scalar_prefetch=1,
            grid=(1,),
            in_specs=[
                pl.BlockSpec((TOK, D), lambda i, s: (0, 0)),
                pl.BlockSpec((4 * TOP, TOK), lambda i, s: (0, 0)),
            ],
            out_specs=[pl.BlockSpec(s, lambda i, _, n=len(s): (0,) * n) for s in shapes],
        ),
        out_shape=[jax.ShapeDtypeStruct(s, jnp.bfloat16) for s in shapes],
        compiler_params=pltpu.CompilerParams(vmem_limit_bytes=VMEM),
    )(targets, grad, meta)


def return_route_kernel(scalars, meta_ref, out_ref):
    core = scalars[0]
    blocks = []
    for i in range(8):
        lines = [meta_ref[i, k : k + 1, :] for k in range(2 * TOP)]
        blocks += [(lines, scalars[1]), (lines, scalars[2])]
    for n, gate in enumerate(slot_weights(blocks)):
        none = jnp.zeros_like(gate)
        both = jnp.concatenate(
            [jnp.where(core == 0, gate, none), jnp.where(core == 1, gate, none)], axis=0
        )
        out_ref[n // 2, n % 2] = both.astype(jnp.bfloat16)


def return_route(scalars, meta):
    return pl.pallas_call(
        return_route_kernel,
        grid_spec=pltpu.PrefetchScalarGridSpec(
            num_scalar_prefetch=1,
            grid=(1,),
            in_specs=[pl.BlockSpec((8, 2 * TOP, TOK), lambda i, s: (0, 0, 0))],
            out_specs=pl.BlockSpec((8, 2, PAIR, TOK), lambda i, s: (0, 0, 0, 0)),
        ),
        out_shape=jax.ShapeDtypeStruct((8, 2, PAIR, TOK), jnp.bfloat16),
        compiler_params=pltpu.CompilerParams(vmem_limit_bytes=VMEM),
    )(scalars, meta)


def combine_kernel(scalars, weight_ref, own_ref, sib_ref, *out_refs, outs):
    chunk = 1024
    for at in range(0, D, chunk):
        total = jnp.zeros((TOK, chunk), jnp.float32)
        for j, rows in enumerate((own_ref, sib_ref)):
            total += lax.dot_general(
                weight_ref[0, j],
                rows[:, at : at + chunk],
                (((0,), (0,)), ((), ())),
                preferred_element_type=jnp.float32,
            )
        for (low, high), ref in zip(outs, out_refs):
            if low <= at < high:
                ref[0, :, at - low : at - low + chunk] = total.astype(jnp.bfloat16)


def combine(pairs, weights, own, sib, first, steps, outs):
    out_specs = [pl.BlockSpec((1, TOK, high - low), lambda i, s: (i, 0, 0)) for low, high in outs]
    return pl.pallas_call(
        functools.partial(combine_kernel, outs=outs),
        grid_spec=pltpu.PrefetchScalarGridSpec(
            num_scalar_prefetch=1,
            grid=(steps,),
            in_specs=[
                pl.BlockSpec((1, 2, PAIR, TOK), lambda i, s: (first + i, 0, 0, 0)),
                pl.BlockSpec((PAIR, D), lambda i, s: (s[first + i], 0)),
                pl.BlockSpec((PAIR, D), lambda i, s: (s[first + i], 0)),
            ],
            out_specs=out_specs,
        ),
        out_shape=[
            jax.ShapeDtypeStruct((steps, TOK, high - low), jnp.bfloat16) for low, high in outs
        ],
        compiler_params=pltpu.CompilerParams(vmem_limit_bytes=VMEM),
    )(pairs, weights, own, sib)


def sent_kernel(scalars, order_ref, *refs):
    tok_refs, out_refs = refs[:QUAD], refs[QUAD:]
    for g in range(STEP):
        sent_rows(scalars, order_ref, [ref.at[g] for ref in tok_refs], [ref.at[g] for ref in out_refs])


def sent_rows(scalars, order_ref, tok_refs, out_refs):
    tokens = jnp.concatenate([ref[:TOK, :] for ref in tok_refs], axis=0)
    blocks = []
    for j in range(2):
        for ref in tok_refs:
            table = ref[TOK:, :TOK].astype(jnp.float32)
            blocks.append(([table[k : k + 1, :] for k in range(2 * TOP)], scalars[j]))
    gates = slot_weights(blocks)
    none = jnp.zeros((SLOT, TOK), jnp.float32)
    for j, out_ref in enumerate(out_refs):
        route = [
            jnp.concatenate(
                [gates[j * QUAD + i] if i == n else none for n in range(QUAD)], axis=1
            )
            for i in range(QUAD)
        ]
        route = jnp.concatenate(route, axis=0).astype(jnp.bfloat16)
        route = jnp.dot(order_ref[...], route, preferred_element_type=jnp.float32)
        sent = jnp.dot(route.astype(jnp.bfloat16), tokens, preferred_element_type=jnp.float32)
        for e in range(E):
            out_ref[e] = sent[e * SLOT : (e + 1) * SLOT, :].astype(jnp.bfloat16)


def build_sent(scalars, order, tokens):
    rows = (NDP, E, SLOT, COLS)
    return pl.pallas_call(
        sent_kernel,
        grid_spec=pltpu.PrefetchScalarGridSpec(
            num_scalar_prefetch=1,
            grid=(NDP // STEP,),
            in_specs=[pl.BlockSpec((QUAD * SLOT, QUAD * SLOT), lambda g, s: (0, 0))]
            + [pl.BlockSpec((STEP, LONG, COLS), lambda g, s: (g, 0, 0)) for _ in range(QUAD)],
            out_specs=[pl.BlockSpec((STEP,) + rows[1:], lambda g, s: (g, 0, 0, 0))] * 2,
        ),
        out_shape=[jax.ShapeDtypeStruct(rows, jnp.bfloat16)] * 2,
        compiler_params=pltpu.CompilerParams(vmem_limit_bytes=VMEM),
        cost_estimate=pl.CostEstimate(
            flops=14_000_000_000, bytes_accessed=15_000_000, transcendentals=0
        ),
    )(scalars, order, *tokens)


def weight_kernel(*refs, counts):
    sent_refs, refs = refs[:4], refs[4:]
    hidden = []
    for count in counts:
        part, refs = refs[:count], refs[count:]
        if count == 2:
            hidden.append(jnp.where(pl.program_id(0) < E // 2, part[0][0], part[1][0]))
        else:
            hidden.append(part[0][0])
    hidden = jnp.concatenate(hidden, axis=0)
    sent = [ref[g, 0].astype(jnp.float32) for g in range(BATCH) for ref in sent_refs]
    sent = jnp.concatenate(sent, axis=0).astype(jnp.bfloat16)
    total = lax.dot_general(
        hidden, sent, (((0,), (0,)), ((), ())), preferred_element_type=jnp.float32
    )
    if len(refs) > 1:
        total += refs[0][0]
    refs[-1][0] = total


def weight_grad(sents, batch, sources, before):
    result = pl.BlockSpec((1, FFW, COLS), lambda e: (e, 0, 0))
    whole = pl.BlockSpec((1, ROWS, FFW), lambda e: (e, 0, 0))
    halves = [
        pl.BlockSpec((1, ROWS, FFW), lambda e: (jnp.minimum(e, E // 2 - 1), 0, 0)),
        pl.BlockSpec((1, ROWS, FFW), lambda e: (jnp.maximum(e - E // 2, 0), 0, 0)),
    ]
    specs = [spec for s in sources for spec in (halves if len(s) == 2 else [whole])]
    return pl.pallas_call(
        functools.partial(weight_kernel, counts=tuple(len(s) for s in sources)),
        grid=(E,),
        in_specs=[pl.BlockSpec((BATCH, 1, SLOT, COLS), lambda e: (batch, e, 0, 0))] * 4
        + specs
        + [result] * len(before),
        out_specs=result,
        out_shape=jax.ShapeDtypeStruct((E, FFW, COLS), jnp.float32),
        compiler_params=pltpu.CompilerParams(vmem_limit_bytes=VMEM),
        cost_estimate=pl.CostEstimate(
            flops=11_000_000_000, bytes_accessed=20_000_000, transcendentals=0
        ),
    )(*sents, *[a for s in sources for a in s], *before)


def local(
    grad_next, gate_next, expert_ids_next, hidden_next, slot_grads, gate_prev, expert_ids_prev
):
    me = lax.axis_index("expert")
    zl, x, c = me // (2 * X), (me // 2) % X, me % 2
    dp = lax.axis_index("dp")
    y, zh = dp // 2, dp % 2
    first = (me * E).astype(jnp.int32)

    def after(value, *earlier):
        return lax.optimization_barrier((value, earlier))[0]

    meta = jnp.concatenate(
        [
            expert_ids_prev.astype(jnp.float32),
            gate_prev,
            expert_ids_next.astype(jnp.float32),
            gate_next,
        ],
        axis=1,
    ).T

    targets = [((y - dy) % 4) * 2 + z for z in (zh, 1 - zh) for dy in range(4)]
    same, other = cut_columns(jnp.stack(targets).astype(jnp.int32), grad_next, meta)
    other = dp_from(other, 0, 1)

    meta = meta[: 2 * TOP]
    meta = jnp.stack([meta, ex_from(meta, 1, 0, 0)])
    meta = jnp.stack([meta] + [ex_from(meta, 0, dx, 0) for dx in (1, 2, 3)])
    meta_prev = meta.reshape(8, 2 * TOP, TOK)

    sibling = ex_from(slot_grads, 0, 0, 1)
    weights = return_route(
        jnp.stack([c, first, (me ^ 1) * E]).astype(jnp.int32), meta_prev
    )
    pairs = jnp.stack(
        [(zl ^ dzl) * X + (x + dx) % X for dx in range(X) for dzl in range(2)]
    ).astype(jnp.int32)
    halves = [(0, HALF), (HALF, D)]

    def part(dx):
        return combine(pairs, weights, slot_grads, sibling, 2 * dx, 2, halves)

    def add(*values):
        return sum(v.astype(jnp.float32) for v in values).astype(jnp.bfloat16)

    blocks = jnp.stack(
        [
            ((zl ^ dzl) * X + (x + dx) % X) * 2 + (c ^ dc)
            for dzl in range(2)
            for dc in range(2)
            for dx in range(X)
        ]
    ).reshape(1, NEX, 1)
    source = (
        blocks * SLOT
        + jnp.arange(E, dtype=jnp.int32)[:, None, None] * CAP
        + jnp.arange(CAP, dtype=jnp.int32)[None, None, :]
    ).reshape(-1)
    move = (source[:, None] == jnp.arange(NEX * SLOT, dtype=jnp.int32)[None, :]).astype(
        jnp.bfloat16
    )
    mine = jnp.dot(move, hidden_next, preferred_element_type=jnp.float32).astype(jnp.bfloat16)
    mine = mine.reshape(E, ROWS, FFW)

    left, right = part(2)
    both = after(jnp.stack([same, other], axis=1), left, right)
    own = [both[0]] + [dp_from(both[dy], dy, 0) for dy in (1, 2, 3)]
    left, right = ex_from(left, 0, 3, 0), ex_from(right, 0, 1, 0)
    up, down, here = part(1), part(3), part(0)
    own = after(own, left, right, *up, *down, *here)
    own = jnp.stack(own, axis=1).reshape(NDP, LONG, COLS)
    up = [add(up[0], left), up[1]]
    down = [down[0], add(down[1], right)]

    def to_sides(zero):
        return dp_from(zero, 1, 0), dp_from(zero, 3, 0)

    mine_low, mine_high = mine[: E // 2], mine[E // 2 :]
    low_near = to_sides(after(mine_low, own))
    high_near = to_sides(after(mine_high, *low_near))
    near_onward = after((low_near[0], high_near[1]), *low_near, *high_near)
    near_onward = dp_from(near_onward[0], 1, 0), dp_from(near_onward[1], 3, 0)

    over = ex_from(own, 1, 0, 0)
    across_low = dp_from(after(mine_low, over), 0, 1)
    near = [own, ex_from(own, 0, 1, 0), None, ex_from(own, 0, 3, 0)]
    near[2] = jnp.concatenate(
        [
            ex_from(after(near[1][:BATCH], over, *up, *down, *low_near), 0, 1, 0),
            ex_from(after(near[3][BATCH:], over, *up, *down, *low_near), 0, 3, 0),
        ]
    )
    to = jnp.arange(QUAD * SLOT, dtype=jnp.int32)
    block_row = to % SLOT // CAP * SLOT + to // SLOT * CAP + to % CAP
    order = (block_row[:, None] == to[None, :]).astype(jnp.bfloat16)
    both_first = jnp.stack([first, (me ^ 1) * E]).astype(jnp.int32)

    def slot_rows(tokens):
        mine_rows, theirs = build_sent(both_first, order, tokens)
        return [mine_rows, ex_from(theirs, 0, 0, 1)]

    sents = slot_rows(after(near, *high_near))
    over_late = after(over, near[2])
    far = [
        over,
        ex_from(over_late, 0, 1, 0),
        ex_from(after(near[2], across_low), 1, 0, 0),
        ex_from(over_late, 0, 3, 0),
    ]

    across_high = dp_from(after(mine_high, far[2]), 0, 1)
    low_far = to_sides(after(across_low, *near_onward))
    high_far = to_sides(after(across_high, *low_far))
    far_onward = after((low_far[0], high_far[1]), *low_far, *high_far)
    far_onward = dp_from(far_onward[0], 1, 0), dp_from(far_onward[1], 3, 0)

    crossed = []
    gates = [(far[1], far[3], *near_onward), low_far]
    for i in range(2):
        if i:
            sents = sents + slot_rows(far)
        u = ex_from(after(up[i], *gates[i], *sents), 0, 3, 0)
        d = ex_from(after(down[i], *gates[i], *sents), 0, 1, 0)
        gates[1] += (u, d)
        side = add(here[i][1], u[1], d[1])
        if i:
            sources = [(mine_low, mine_high), *zip(low_near, high_near)]
            sources.insert(2, near_onward)
            down_grad = weight_grad(sents, 0, sources, [])
            side = after(side, down_grad, *high_far)
        side = ex_from(side, 1, 0, 0)
        crossed.append(add(here[i][0], u[0], d[0], side))
    input_grad = jnp.concatenate(crossed, axis=1)
    sources = [(across_low, across_high), *zip(low_far, high_far)]
    sources.insert(2, far_onward)
    down_grad = weight_grad(sents, 1, sources, [down_grad])
    return down_grad, input_grad


def solution(mesh):
    rows = P(("dp", "expert"), None)
    return jax.shard_map(
        local,
        mesh=mesh,
        in_specs=(rows,) * 7,
        out_specs=(P("expert", None, "dp"), rows),
        check_vma=False,
    )
```
